32 devices in a mesh: slab: 8 (over z, y), chan: 4 (over x, core).
Axes of the slice: x: 2, y: 2, z: 4, core: 2. Of those that a mesh axis runs over, the one named last changes fastest.
Arguments:
- state_field: bfloat16 [2, 16, 256, 256, 256], P(None, 'chan', 'slab'), may hold values from -6 to 6
- spectral_weights: bfloat16 [16, 16, 64, 32, 2, 64], P(None, None, 'chan', None, None, 'slab'), may hold values from -1 to 1
- channel_shift: bfloat16 [16], P('chan'), may hold values from -3 to 3
Outputs:
- layer_output: bfloat16 [2, 16, 256, 256, 256], P(None, 'chan', 'slab')
The draws below stay inside these ranges and needn't reach their ends.
All inputs are finite; a program needn't handle non-finite values.
Results may differ from the reference program's by a relative error of at most 0.015.
Values may be sent and summed in bfloat16 or wider, within the bound.
No kernel may reach another device: no remote copies, remote signals or barrier semaphores. Data moves between devices by JAX's collectives and lax.ppermute only.
A program may use at most 192 MiB of HBM per device.

```python
import jax
import jax.numpy as jnp
from jax import lax

NG = 256
CH = 16
KM = 32
SAMPLES = 2


def shard_levels(key, dims, pieces, low, top_value):
    factor_of = 1.0
    for axis_at, blocks in pieces:
        draws = jax.random.uniform(jax.random.fold_in(jax.random.fold_in(key, 6), axis_at), (blocks,), jnp.float32, low / len(pieces), top_value / len(pieces))
        factor_of = factor_of * jnp.repeat(jnp.exp(draws), dims[axis_at] // blocks).reshape((-1,) + (1,) * (len(dims) - 1 - axis_at))
    return factor_of


def centred(own_key, extent, scale, reach, pieces=(), kind=jnp.bfloat16):
    factor_of = shard_levels(own_key, extent, pieces, -0.22, 0.18) if pieces else 1.0
    entries = jax.random.normal(own_key, extent, jnp.float32) * scale * factor_of
    return jnp.minimum(jnp.maximum(entries, -reach), reach).astype(kind)


def setup_inputs(seed: int = 0) -> dict:
    keys = jax.random.split(jax.random.key(seed), 4)
    state_field = centred(keys[0], (SAMPLES, CH, NG, NG, NG), 1.0, 6.0, ((1, 4), (2, 8)))
    spectral_weights = centred(keys[1], (CH, CH, 2 * KM, KM, 2, 2 * KM), (2 * CH) ** -0.5, 1.0, ((2, 4), (5, 8)))
    channel_shift = centred(keys[2], (CH,), 0.5, 3.0, ((0, 4),))
    return {"state_field": state_field, "spectral_weights": spectral_weights, "channel_shift": channel_shift}


def kept_freqs(mode_count, grid_side):
    index = jnp.arange(mode_count, dtype=jnp.int32)
    return jnp.where(index < mode_count // 2, index, index + grid_side - mode_count)

def angles(freq_list, grid_side):
    places = jnp.arange(grid_side, dtype=jnp.int32)
    product = freq_list[:, None] * places[None, :] % grid_side
    return product.astype(jnp.float32) * (2.0 * jnp.pi / grid_side)

def make_tables(grid_side, kept):
    bf = jnp.bfloat16
    fwd_scale = 1.0 / jnp.sqrt(jnp.float32(grid_side))
    inv_scale = 1.0 / jnp.sqrt(jnp.float32(2 * kept))
    z_freqs = jnp.arange(kept, dtype=jnp.int32)
    two_freqs = kept_freqs(2 * kept, grid_side)
    theta_z = angles(z_freqs, grid_side)
    theta_two = angles(two_freqs, grid_side)
    cos_z = jnp.cos(theta_z).T
    sin_z = jnp.sin(theta_z).T
    table_z = (jnp.stack([cos_z, -sin_z], -1) * fwd_scale).astype(bf)
    cos_t = jnp.cos(theta_two).T
    sin_t = jnp.sin(theta_two).T
    table_y = (jnp.stack([jnp.stack([cos_t, -sin_t], 1), jnp.stack([sin_t, cos_t], 1)], 0) * fwd_scale).astype(bf)
    table_x = (jnp.stack([jnp.stack([cos_t, -sin_t], -1), jnp.stack([sin_t, cos_t], -1)], 1) * fwd_scale).astype(bf)
    cos_m = jnp.cos(theta_two)
    sin_m = jnp.sin(theta_two)
    inv_x = (jnp.stack([jnp.stack([cos_m, sin_m], -1), jnp.stack([-sin_m, cos_m], -1)], 1) * inv_scale).astype(bf)
    inv_y = (jnp.stack([jnp.stack([cos_m, sin_m], 1), jnp.stack([-sin_m, cos_m], 1)], 0) * inv_scale).astype(bf)
    weight_k = jnp.where(z_freqs == 0, 1.0, 2.0).astype(jnp.float32)[:, None]
    inv_z = (jnp.stack([weight_k * jnp.cos(theta_z), -weight_k * jnp.sin(theta_z)], 1) * inv_scale).astype(bf)
    return (table_z, table_y, table_x, inv_x, inv_y, inv_z)

def reference(state_field, spectral_weights, channel_shift):
    f32 = jnp.float32
    bf = jnp.bfloat16
    table_z, table_y, table_x, inv_x, inv_y, inv_z = make_tables(NG, KM)
    flat_grids = state_field.reshape(SAMPLES * CH, NG, NG, NG)

    def forward_one(one_grid):
        coef_z = jnp.einsum('xyz,zkp->xkpy', one_grid.astype(f32), table_z.astype(f32)).astype(bf)
        coef_y = jnp.einsum('xkpy,pyqn->xkqn', coef_z.astype(f32), table_y.astype(f32)).astype(bf)
        coef_x = jnp.einsum('xkpn,xpmq->mkqn', coef_y.astype(f32), table_x.astype(f32)).astype(bf)
        return coef_x
    spectra = lax.map(forward_one, flat_grids).reshape(SAMPLES, CH, 2 * KM, KM, 2, 2 * KM)
    spec_re = spectra[..., 0, :].astype(f32)
    spec_im = spectra[..., 1, :].astype(f32)
    wgt_re = spectral_weights[..., 0, :].astype(f32)
    wgt_im = spectral_weights[..., 1, :].astype(f32)
    mixed_re = jnp.einsum('bimkj,iomkj->bomkj', spec_re, wgt_re) - jnp.einsum('bimkj,iomkj->bomkj', spec_im, wgt_im)
    mixed_im = jnp.einsum('bimkj,iomkj->bomkj', spec_re, wgt_im) + jnp.einsum('bimkj,iomkj->bomkj', spec_im, wgt_re)
    mixed = jnp.stack([mixed_re, mixed_im], -2).astype(bf)
    flat_mixed = mixed.reshape(SAMPLES * CH, 2 * KM, KM, 2, 2 * KM)
    shifts = jnp.tile(channel_shift, SAMPLES)

    def inverse_one(packed):
        one_spec, shift_value = packed
        split_spec = one_spec.astype(f32)
        back_x = jnp.einsum('mkpn,mpxq->xkqn', split_spec, inv_x.astype(f32)).astype(bf)
        back_y = jnp.einsum('xkpn,pnqy->xkqy', back_x.astype(f32), inv_y.astype(f32)).astype(bf)
        summed = jnp.einsum('xkpy,kpz->xyz', back_y.astype(f32), inv_z.astype(f32))
        return jax.nn.gelu(summed + shift_value.astype(f32), approximate=False).astype(bf)
    result = lax.map(inverse_one, (flat_mixed, shifts))
    return result.reshape(SAMPLES, CH, NG, NG, NG)
```

```python
import functools

import jax
import jax.numpy as jnp
import numpy as np
from jax import lax
from jax.experimental import pallas as pl
from jax.experimental.pallas import tpu as pltpu
from jax.sharding import PartitionSpec as P

NG = 256
KM = 32
F32 = jnp.float32
BF16 = jnp.bfloat16
VMEM_LIMIT = 48 * 1024 * 1024


def kept_freqs(mode_count, grid_side):
    index = np.arange(mode_count)
    return np.where(index < mode_count // 2, index, index + grid_side - mode_count)


def angles(freq_list, grid_side):
    product = freq_list[:, None] * np.arange(grid_side)[None, :] % grid_side
    return product.astype(np.float32) * np.float32(2.0 * np.pi / grid_side)


def make_tables(chans):
    two = 2 * KM
    fwd = np.float32(1.0) / np.sqrt(np.float32(NG))
    inv = np.float32(1.0) / np.sqrt(np.float32(two))
    theta_z = angles(np.arange(KM), NG)
    theta_two = angles(kept_freqs(two, NG), NG)
    cos_z, sin_z = np.cos(theta_z), np.sin(theta_z)
    cos_t, sin_t = np.cos(theta_two), np.sin(theta_two)
    lanes = 2 * chans * KM
    fwd_z = np.zeros((chans, NG, 2, chans, KM), np.float32)
    inv_z = np.zeros((chans, 2, chans, KM, NG), np.float32)
    weight_k = np.where(np.arange(KM) == 0, 1.0, 2.0).astype(np.float32)[:, None]
    for c in range(chans):
        fwd_z[c, :, 0, c, :] = cos_z.T * fwd
        fwd_z[c, :, 1, c, :] = -sin_z.T * fwd
        inv_z[c, 0, c] = weight_k * cos_z * inv
        inv_z[c, 1, c] = -weight_k * sin_z * inv
    fwd_z = fwd_z.reshape(chans * NG, lanes)
    inv_z = inv_z.reshape(chans, lanes, NG)
    fwd_two = np.concatenate([cos_t, sin_t], 0) * fwd
    inv_two = np.concatenate([cos_t.T, sin_t.T], 1) * inv
    return tuple(jnp.asarray(t, BF16) for t in (fwd_z, fwd_two, inv_two, inv_z))


def dot(a, b):
    return jnp.dot(a, b, preferred_element_type=F32)


def turn(rows):
    half = rows.shape[-1] // 2
    return jnp.concatenate([-rows[:, half:], rows[:, :half]], axis=1)


def unturn(twice):
    two, half = twice.shape[0] // 2, twice.shape[1] // 2
    cos_part, sin_part = twice[:two], twice[two:]
    return jnp.concatenate(
        [cos_part[:, :half] + sin_part[:, half:], cos_part[:, half:] - sin_part[:, :half]], axis=1
    )


def call(kernel, cost, **kwargs):
    flops, moved = cost
    return pl.pallas_call(
        kernel,
        compiler_params=pltpu.CompilerParams(vmem_limit_bytes=VMEM_LIMIT),
        cost_estimate=pl.CostEstimate(flops=flops, bytes_accessed=moved, transcendentals=0),
        **kwargs,
    )


def forward_zy(state, sample, slabs, fwd_z, fwd_two):
    _, chans, planes, _, _ = state.shape
    two = fwd_two.shape[0] // 2
    own = two // slabs
    lanes = fwd_z.shape[1]
    step = max(4, 16 // own)

    def kernel(state_ref, fwd_z_ref, fwd_two_ref, out_ref):
        found = []
        for x in range(step):
            plane = jnp.concatenate([state_ref[0, c, x] for c in range(chans)], axis=1)
            coef_z = dot(plane, fwd_z_ref[...]).astype(BF16)
            found.append(unturn(dot(fwd_two_ref[...], coef_z)).reshape(slabs, own, lanes))
        rows = jnp.stack(found, axis=1).reshape(slabs, step * own, lanes)
        out_ref[...] = rows.astype(BF16)

    return call(
        kernel,
        (2 * planes * NG * lanes * (chans * NG + 2 * two), 2 * chans * planes * NG * NG),
        grid=(planes // step,),
        in_specs=[
            pl.BlockSpec((1, chans, step, NG, NG), lambda i: (sample, 0, i, 0, 0)),
            pl.BlockSpec(fwd_z.shape, lambda i: (0, 0)),
            pl.BlockSpec(fwd_two.shape, lambda i: (0, 0)),
        ],
        out_specs=pl.BlockSpec((slabs, step * own, lanes), lambda i: (0, i, 0)),
        out_shape=jax.ShapeDtypeStruct((slabs, planes * own, lanes), BF16),
        name="forward_zy",
    )(state, fwd_z, fwd_two)


def forward_x(coef_y, groups, fwd_two):
    slabs, rows, lanes = coef_y.shape
    two = fwd_two.shape[0] // 2
    own = two // slabs
    half = lanes // 2
    part = two // groups

    def kernel(coef_ref, table_ref, out_ref, wide, found):
        flat = coef_ref[...].reshape(slabs * rows, lanes).astype(F32)
        wide[0] = flat[:, :half]
        wide[1] = flat[:, half:]
        for n in range(own):
            pick = pl.ds(n, NG, stride=own)
            planes = jnp.concatenate([wide[0, pick, :], wide[1, pick, :]], axis=1)
            modes = unturn(dot(table_ref[...], planes.astype(BF16)))
            put = pl.ds(n, two, stride=own)
            found[0, put, :] = modes[:, :half]
            found[1, put, :] = modes[:, half:]
        both = jnp.concatenate([found[0], found[1]], axis=1)
        out_ref[...] = both.reshape(groups, part * own, lanes).astype(BF16)

    return call(
        kernel,
        (4 * own * two * NG * lanes, 4 * slabs * rows * lanes),
        in_specs=[pl.BlockSpec(memory_space=pltpu.VMEM)] * 2,
        out_specs=pl.BlockSpec(memory_space=pltpu.VMEM),
        out_shape=jax.ShapeDtypeStruct((groups, part * own, lanes), BF16),
        scratch_shapes=[
            pltpu.VMEM((2, slabs * rows, half), F32),
            pltpu.VMEM((2, two * own, half), F32),
        ],
        name="forward_x",
    )(coef_y, fwd_two)


def place_weights(weights, chans):
    inputs, outputs, modes, _, own, kept = weights.shape
    groups = inputs // chans
    rows = modes * own
    lanes = chans * kept

    def kernel(w_ref, out_ref):
        for q in range(2):
            tiles = {}
            for i in range(chans):
                for o in range(chans):
                    tiles[i, o] = w_ref[i, o, :, q].astype(F32).reshape(rows, kept)
            for r in range(chans):
                row = jnp.concatenate([tiles[(o + r) % chans, o] for o in range(chans)], axis=1)
                out_ref[q, 0, 0, r] = row.astype(BF16)

    return call(
        kernel,
        (2 * weights.size, 10 * weights.size),
        grid=(groups, outputs // chans),
        in_specs=[
            pl.BlockSpec((chans, chans, modes, 2, own, kept), lambda i, o: (i, o, 0, 0, 0, 0))
        ],
        out_specs=pl.BlockSpec((2, 1, 1, chans, rows, lanes), lambda i, o: (0, i, o, 0, 0, 0)),
        out_shape=jax.ShapeDtypeStruct(
            (2, groups, outputs // chans, chans, rows, lanes), BF16
        ),
        name="place_weights",
    )(weights)


def mix(spectra, placed, kept):
    groups, rows, lanes = spectra.shape
    half = lanes // 2
    chans = placed.shape[3]
    step = 16

    def kernel(spec_ref, w_ref, out_ref):
        total = [[jnp.zeros((step, half), F32) for _ in range(2)] for _ in range(groups)]
        for i in range(groups):
            both = spec_ref[i].astype(F32)
            for r in range(chans):
                if r == 0:
                    re, im = both[:, :half], both[:, half:]
                else:
                    re = pltpu.roll(both[:, :half], half - r * kept, 1)
                    im = pltpu.roll(both[:, half:], half - r * kept, 1)
                for o in range(groups):
                    w_re = w_ref[0, i, o, r].astype(F32)
                    w_im = w_ref[1, i, o, r].astype(F32)
                    total[o][0] = total[o][0] + (re * w_re - im * w_im)
                    total[o][1] = total[o][1] + (re * w_im + im * w_re)
        for o in range(groups):
            out_ref[o] = jnp.concatenate(total[o], axis=1).astype(BF16)

    return call(
        kernel,
        (8 * groups * groups * chans * rows * half, 2 * placed.size),
        grid=(rows // step,),
        in_specs=[
            pl.BlockSpec((groups, step, lanes), lambda t: (0, t, 0)),
            pl.BlockSpec(placed.shape[:4] + (step, half), lambda t: (0, 0, 0, 0, t, 0)),
        ],
        out_specs=pl.BlockSpec((groups, step, lanes), lambda t: (0, t, 0)),
        out_shape=jax.ShapeDtypeStruct(spectra.shape, BF16),
        name="mix",
    )(spectra, placed)


def inverse_x(mixed, slabs, inv_two):
    groups, rows, lanes = mixed.shape
    two = inv_two.shape[1] // 2
    own = groups * rows // two
    half = lanes // 2

    def kernel(mixed_ref, table_ref, out_ref, wide, found):
        flat = mixed_ref[...].reshape(groups * rows, lanes).astype(F32)
        wide[0] = flat[:, :half]
        wide[1] = flat[:, half:]
        for n in range(own):
            pick = pl.ds(n, two, stride=own)
            modes = jnp.concatenate([wide[0, pick, :], wide[1, pick, :]], axis=1)
            twice = jnp.concatenate([modes, turn(modes)], axis=0).astype(BF16)
            planes = dot(table_ref[...], twice)
            put = pl.ds(n, NG, stride=own)
            found[0, put, :] = planes[:, :half]
            found[1, put, :] = planes[:, half:]
        both = jnp.concatenate([found[0], found[1]], axis=1)
        out_ref[...] = both.reshape(slabs, NG * own // slabs, lanes).astype(BF16)

    return call(
        kernel,
        (4 * own * two * NG * lanes, 4 * NG * own * lanes),
        in_specs=[pl.BlockSpec(memory_space=pltpu.VMEM)] * 2,
        out_specs=pl.BlockSpec(memory_space=pltpu.VMEM),
        out_shape=jax.ShapeDtypeStruct((slabs, NG * own // slabs, lanes), BF16),
        scratch_shapes=[
            pltpu.VMEM((2, two * own, half), F32),
            pltpu.VMEM((2, NG * own, half), F32),
        ],
        name="inverse_x",
    )(mixed, inv_two)


def inverse_yz(back_x, shift, sample, shape, filled, inv_two, inv_z):
    slabs, rows, lanes = back_x.shape
    _, chans, planes, _, _ = shape
    two = inv_two.shape[1] // 2
    own = two // slabs
    step = max(2, 16 // own)

    def kernel(back_ref, shift_ref, inv_two_ref, inv_z_ref, *refs):
        out_ref = refs[-1]
        wide = back_ref[...].astype(F32)
        for x in range(step):
            modes = wide[:, x * own : (x + 1) * own, :].reshape(two, lanes)
            twice = jnp.concatenate([modes, turn(modes)], axis=0).astype(BF16)
            back_y = dot(inv_two_ref[...], twice).astype(BF16)
            for c in range(chans):
                shifted = dot(back_y, inv_z_ref[c]) + shift_ref[c]
                half = 0.5 * shifted
                value = half + half * lax.erf(shifted * np.float32(np.sqrt(0.5)))
                out_ref[0, c, x] = value.astype(BF16)

    extra = [] if filled is None else [filled]
    return call(
        kernel,
        (2 * planes * NG * (2 * two * lanes + chans * lanes * NG), 2 * chans * planes * NG * NG),
        grid=(planes // step,),
        in_specs=[
            pl.BlockSpec((slabs, step * own, lanes), lambda i: (0, i, 0)),
            pl.BlockSpec(memory_space=pltpu.SMEM),
            pl.BlockSpec(inv_two.shape, lambda i: (0, 0)),
            pl.BlockSpec(inv_z.shape, lambda i: (0, 0, 0)),
        ]
        + [pl.BlockSpec(memory_space=pl.ANY)] * len(extra),
        out_specs=pl.BlockSpec((1, chans, step, NG, NG), lambda i: (sample, 0, i, 0, 0)),
        out_shape=jax.ShapeDtypeStruct(shape, BF16),
        input_output_aliases={} if filled is None else {4: 0},
        name="inverse_yz",
    )(back_x, shift, inv_two, inv_z, *extra)


def exchange(blocks, axis):
    return lax.all_to_all(blocks, axis, split_axis=0, concat_axis=0, tiled=True)


def on_device(slabs, groups, state, weights, shift):
    samples, chans = state.shape[:2]
    fwd_z, fwd_two, inv_two, inv_z = make_tables(chans)
    shift = shift.astype(F32)
    placed = place_weights(jnp.transpose(weights, (0, 1, 2, 4, 5, 3)), chans)
    out = None
    for b in range(samples):
        coef_y = exchange(forward_zy(state, b, slabs, fwd_z, fwd_two), "slab")
        spectra = exchange(forward_x(coef_y, groups, fwd_two), "chan")
        mixed = exchange(mix(spectra, placed, KM), "chan")
        back_x = exchange(inverse_x(mixed, slabs, inv_two), "slab")
        out = inverse_yz(back_x, shift, b, state.shape, out, inv_two, inv_z)
    return out


def solution(mesh):
    slabs, groups = mesh.shape["slab"], mesh.shape["chan"]
    return jax.shard_map(
        functools.partial(on_device, slabs, groups),
        mesh=mesh,
        in_specs=(
            P(None, "chan", "slab", None, None),
            P(None, None, "chan", None, None, "slab"),
            P("chan"),
        ),
        out_specs=P(None, "chan", "slab", None, None),
        check_vma=False,
    )
```

```python
import functools

import jax
import jax.numpy as jnp
import numpy as np
from jax import lax
from jax.experimental import pallas as pl
from jax.experimental.pallas import tpu as pltpu
from jax.sharding import PartitionSpec as P

NG = 256
KM = 32
F32 = jnp.float32
BF16 = jnp.bfloat16
VMEM_LIMIT = 48 * 1024 * 1024


def kept_freqs(mode_count, grid_side):
    index = np.arange(mode_count)
    return np.where(index < mode_count // 2, index, index + grid_side - mode_count)


def angles(freq_list, grid_side):
    product = freq_list[:, None] * np.arange(grid_side)[None, :] % grid_side
    return product.astype(np.float32) * np.float32(2.0 * np.pi / grid_side)


def make_tables(chans):
    two = 2 * KM
    fwd = np.float32(1.0) / np.sqrt(np.float32(NG))
    inv = np.float32(1.0) / np.sqrt(np.float32(two))
    theta_z = angles(np.arange(KM), NG)
    theta_two = angles(kept_freqs(two, NG), NG)
    cos_z, sin_z = np.cos(theta_z), np.sin(theta_z)
    cos_t, sin_t = np.cos(theta_two), np.sin(theta_two)
    lanes = 2 * chans * KM
    fwd_z = np.zeros((chans, NG, 2, chans, KM), np.float32)
    inv_z = np.zeros((chans, 2, chans, KM, NG), np.float32)
    weight_k = np.where(np.arange(KM) == 0, 1.0, 2.0).astype(np.float32)[:, None]
    for c in range(chans):
        fwd_z[c, :, 0, c, :] = cos_z.T * fwd
        fwd_z[c, :, 1, c, :] = -sin_z.T * fwd
        inv_z[c, 0, c] = weight_k * cos_z * inv
        inv_z[c, 1, c] = -weight_k * sin_z * inv
    fwd_z = fwd_z.reshape(chans * NG, lanes)
    inv_z = inv_z.reshape(chans, lanes, NG)
    fwd_two = np.concatenate([cos_t, sin_t], 0) * fwd
    inv_two = np.concatenate([cos_t.T, sin_t.T], 1) * inv
    return tuple(jnp.asarray(t, BF16) for t in (fwd_z, fwd_two, inv_two, inv_z))


def dot(a, b):
    return jnp.dot(a, b, preferred_element_type=F32)


def turn(rows):
    half = rows.shape[-1] // 2
    return jnp.concatenate([-rows[:, half:], rows[:, :half]], axis=1)


def unturn(twice):
    two, half = twice.shape[0] // 2, twice.shape[1] // 2
    cos_part, sin_part = twice[:two], twice[two:]
    return jnp.concatenate(
        [cos_part[:, :half] + sin_part[:, half:], cos_part[:, half:] - sin_part[:, :half]], axis=1
    )


def call(kernel, cost, **kwargs):
    flops, moved = cost
    return pl.pallas_call(
        kernel,
        compiler_params=pltpu.CompilerParams(vmem_limit_bytes=VMEM_LIMIT),
        cost_estimate=pl.CostEstimate(flops=flops, bytes_accessed=moved, transcendentals=0),
        **kwargs,
    )


def forward_zy(state, sample, slabs, fwd_z, fwd_two):
    _, chans, planes, _, _ = state.shape
    two = fwd_two.shape[0] // 2
    own = two // slabs
    lanes = fwd_z.shape[1]
    step = min(planes, max(8, 16 // own))

    def kernel(state_ref, fwd_z_ref, fwd_two_ref, out_ref, coef_z):
        for x in range(step):
            plane = jnp.concatenate([state_ref[0, c, x] for c in range(chans)], axis=1)
            coef_z[x] = dot(plane, fwd_z_ref[...]).astype(BF16)
        found = []
        for x in range(step):
            modes = unturn(dot(fwd_two_ref[...], coef_z[x]))
            found.append(modes.reshape(slabs, own, lanes))
        rows = jnp.stack(found, axis=1).reshape(slabs, step * own, lanes)
        out_ref[...] = rows.astype(BF16)

    return call(
        kernel,
        (2 * planes * NG * lanes * (chans * NG + 2 * two), 2 * chans * planes * NG * NG),
        grid=(planes // step,),
        in_specs=[
            pl.BlockSpec((1, chans, step, NG, NG), lambda i: (sample, 0, i, 0, 0)),
            pl.BlockSpec(fwd_z.shape, lambda i: (0, 0)),
            pl.BlockSpec(fwd_two.shape, lambda i: (0, 0)),
        ],
        out_specs=pl.BlockSpec((slabs, step * own, lanes), lambda i: (0, i, 0)),
        out_shape=jax.ShapeDtypeStruct((slabs, planes * own, lanes), BF16),
        scratch_shapes=[pltpu.VMEM((step, NG, lanes), BF16)],
        name="forward_zy",
    )(state, fwd_z, fwd_two)


def forward_x(coef_y, me, groups, fwd_two):
    slabs, rows, lanes = coef_y.shape
    two = fwd_two.shape[0] // 2
    own = two // slabs
    half = lanes // 2
    part = two // groups

    def kernel(me_ref, coef_ref, table_ref, *refs):
        wide, found = refs[groups:]
        flat = coef_ref[...].reshape(slabs * rows, lanes).astype(F32)
        wide[0] = flat[:, :half]
        wide[1] = flat[:, half:]
        for n in range(own):
            pick = pl.ds(n, NG, stride=own)
            planes = jnp.concatenate([wide[0, pick, :], wide[1, pick, :]], axis=1)
            modes = unturn(dot(table_ref[...], planes.astype(BF16)))
            put = pl.ds(n, two, stride=own)
            found[0, put, :] = modes[:, :half]
            found[1, put, :] = modes[:, half:]
        for r in range(groups):
            start = pl.multiple_of((me_ref[0] ^ r) * part * own, part * own)
            pick = pl.ds(start, part * own)
            both = jnp.concatenate([found[0, pick, :], found[1, pick, :]], axis=1)
            refs[r][...] = both.astype(BF16)

    return call(
        kernel,
        (4 * own * two * NG * lanes, 4 * slabs * rows * lanes),
        in_specs=[pl.BlockSpec(memory_space=pltpu.SMEM)]
        + [pl.BlockSpec(memory_space=pltpu.VMEM)] * 2,
        out_specs=[pl.BlockSpec(memory_space=pltpu.VMEM)] * groups,
        out_shape=[jax.ShapeDtypeStruct((part * own, lanes), BF16)] * groups,
        scratch_shapes=[
            pltpu.VMEM((2, slabs * rows, half), F32),
            pltpu.VMEM((2, two * own, half), F32),
        ],
        name="forward_x",
    )(me, coef_y, fwd_two)


def place_weights(weights, me, chans):
    inputs, outputs, modes, _, own, kept = weights.shape
    groups = inputs // chans
    rows = modes * own
    lanes = chans * kept

    def kernel(me_ref, w_ref, out_ref):
        for q in range(2):
            tiles = {}
            for i in range(chans):
                for o in range(chans):
                    tiles[i, o] = w_ref[i, o, :, q].astype(F32).reshape(rows, kept)
            for r in range(chans):
                row = jnp.concatenate([tiles[(o + r) % chans, o] for o in range(chans)], axis=1)
                out_ref[q, 0, 0, r] = row.astype(BF16)

    return call(
        kernel,
        (2 * weights.size, 10 * weights.size),
        grid_spec=pltpu.PrefetchScalarGridSpec(
            num_scalar_prefetch=1,
            grid=(groups, outputs // chans),
            in_specs=[
                pl.BlockSpec(
                    (chans, chans, modes, 2, own, kept),
                    lambda i, o, me_ref: (me_ref[0] ^ i, me_ref[0] ^ o, 0, 0, 0, 0),
                )
            ],
            out_specs=pl.BlockSpec(
                (2, 1, 1, chans, rows, lanes), lambda i, o, me_ref: (0, i, o, 0, 0, 0)
            ),
        ),
        out_shape=jax.ShapeDtypeStruct(
            (2, groups, outputs // chans, chans, rows, lanes), BF16
        ),
        name="place_weights",
    )(me, weights)


def mix(spectra, placed, kept):
    groups = len(spectra)
    rows, lanes = spectra[0].shape
    half = lanes // 2
    chans = placed.shape[3]
    step = min(rows, 32)

    def kernel(w_ref, *refs):
        total = [[jnp.zeros((step, half), F32) for _ in range(2)] for _ in range(groups)]
        for i in range(groups):
            both = refs[i][...].astype(F32)
            for r in range(chans):
                if r == 0:
                    re, im = both[:, :half], both[:, half:]
                else:
                    re = pltpu.roll(both[:, :half], half - r * kept, 1)
                    im = pltpu.roll(both[:, half:], half - r * kept, 1)
                for o in range(groups):
                    w_re = w_ref[0, i, o, r].astype(F32)
                    w_im = w_ref[1, i, o, r].astype(F32)
                    total[o][0] = total[o][0] + (re * w_re - im * w_im)
                    total[o][1] = total[o][1] + (re * w_im + im * w_re)
        for o in range(groups):
            refs[groups + o][...] = jnp.concatenate(total[o], axis=1).astype(BF16)

    return call(
        kernel,
        (8 * groups * groups * chans * rows * half, 2 * placed.size),
        grid=(rows // step,),
        in_specs=[pl.BlockSpec(placed.shape[:4] + (step, half), lambda t: (0, 0, 0, 0, t, 0))]
        + [pl.BlockSpec((step, lanes), lambda t: (t, 0))] * groups,
        out_specs=[pl.BlockSpec((step, lanes), lambda t: (t, 0))] * groups,
        out_shape=[jax.ShapeDtypeStruct((rows, lanes), BF16)] * groups,
        name="mix",
    )(placed, *spectra)


def inverse_x(mixed, me, slabs, inv_two):
    groups = len(mixed)
    rows, lanes = mixed[0].shape
    two = inv_two.shape[1] // 2
    own = groups * rows // two
    half = lanes // 2

    def kernel(me_ref, table_ref, *refs):
        out_ref, wide, found = refs[groups:]
        for r in range(groups):
            put = pl.ds(pl.multiple_of((me_ref[0] ^ r) * rows, rows), rows)
            both = refs[r][...].astype(F32)
            wide[0, put, :] = both[:, :half]
            wide[1, put, :] = both[:, half:]
        for n in range(own):
            pick = pl.ds(n, two, stride=own)
            modes = jnp.concatenate([wide[0, pick, :], wide[1, pick, :]], axis=1)
            twice = jnp.concatenate([modes, turn(modes)], axis=0).astype(BF16)
            planes = dot(table_ref[...], twice)
            put = pl.ds(n, NG, stride=own)
            found[0, put, :] = planes[:, :half]
            found[1, put, :] = planes[:, half:]
        both = jnp.concatenate([found[0], found[1]], axis=1)
        out_ref[...] = both.reshape(slabs, NG * own // slabs, lanes).astype(BF16)

    return call(
        kernel,
        (4 * own * two * NG * lanes, 4 * NG * own * lanes),
        in_specs=[pl.BlockSpec(memory_space=pltpu.SMEM)]
        + [pl.BlockSpec(memory_space=pltpu.VMEM)] * (1 + groups),
        out_specs=pl.BlockSpec(memory_space=pltpu.VMEM),
        out_shape=jax.ShapeDtypeStruct((slabs, NG * own // slabs, lanes), BF16),
        scratch_shapes=[
            pltpu.VMEM((2, two * own, half), F32),
            pltpu.VMEM((2, NG * own, half), F32),
        ],
        name="inverse_x",
    )(me, inv_two, *mixed)


def inverse_yz(back_x, shift, sample, shape, filled, inv_two, inv_z):
    slabs, rows, lanes = back_x.shape
    _, chans, planes, _, _ = shape
    two = inv_two.shape[1] // 2
    own = two // slabs
    step = min(planes, max(8, 16 // own))

    def kernel(back_ref, shift_ref, inv_two_ref, inv_z_ref, *refs):
        out_ref, back_y = refs[-2:]
        wide = back_ref[...].astype(F32)
        for x in range(step):
            modes = wide[:, x * own : (x + 1) * own, :].reshape(two, lanes)
            twice = jnp.concatenate([modes, turn(modes)], axis=0).astype(BF16)
            back_y[x] = dot(inv_two_ref[...], twice).astype(BF16)
        flat = back_y[...].reshape(step * NG, lanes)
        for c in range(chans):
            shifted = dot(flat, inv_z_ref[c]) + shift_ref[c]
            half = 0.5 * shifted
            value = half + half * lax.erf(shifted * np.float32(np.sqrt(0.5)))
            out_ref[0, c] = value.astype(BF16).reshape(step, NG, NG)

    extra = [] if filled is None else [filled]
    return call(
        kernel,
        (2 * planes * NG * (2 * two * lanes + chans * lanes * NG), 2 * chans * planes * NG * NG),
        grid=(planes // step,),
        in_specs=[
            pl.BlockSpec((slabs, step * own, lanes), lambda i: (0, i, 0)),
            pl.BlockSpec(memory_space=pltpu.SMEM),
            pl.BlockSpec(inv_two.shape, lambda i: (0, 0)),
            pl.BlockSpec(inv_z.shape, lambda i: (0, 0, 0)),
        ]
        + [pl.BlockSpec(memory_space=pl.ANY)] * len(extra),
        out_specs=pl.BlockSpec((1, chans, step, NG, NG), lambda i: (sample, 0, i, 0, 0)),
        out_shape=jax.ShapeDtypeStruct(shape, BF16),
        scratch_shapes=[pltpu.VMEM((step, NG, lanes), BF16)],
        input_output_aliases={} if filled is None else {4: 0},
        name="inverse_yz",
    )(back_x, shift, inv_two, inv_z, *extra)


def exchange(blocks, axis):
    return lax.all_to_all(blocks, axis, split_axis=0, concat_axis=0, tiled=True)


def swap(blocks, axis):
    count = len(blocks)
    return list(blocks[:1]) + [
        lax.ppermute(blocks[r], axis, [(i, i ^ r) for i in range(count)]) for r in range(1, count)
    ]


def on_device(slabs, groups, state, weights, shift):
    samples, chans = state.shape[:2]
    fwd_z, fwd_two, inv_two, inv_z = make_tables(chans)
    shift = shift.astype(F32)
    me = lax.axis_index("chan").reshape(1)
    placed = place_weights(jnp.transpose(weights, (0, 1, 2, 4, 5, 3)), me, chans)
    coef_y = [
        exchange(forward_zy(state, b, slabs, fwd_z, fwd_two), "slab") for b in range(samples)
    ]
    coef_y[0], placed = lax.optimization_barrier((coef_y[0], placed))
    back_x = []
    for b in range(samples):
        spectra = swap(forward_x(coef_y[b], me, groups, fwd_two), "chan")
        mixed = swap(mix(spectra, placed, KM), "chan")
        back_x.append(exchange(inverse_x(mixed, me, slabs, inv_two), "slab"))
    out = None
    for b in range(samples):
        out = inverse_yz(back_x[b], shift, b, state.shape, out, inv_two, inv_z)
    return out


def solution(mesh):
    slabs, groups = mesh.shape["slab"], mesh.shape["chan"]
    return jax.shard_map(
        functools.partial(on_device, slabs, groups),
        mesh=mesh,
        in_specs=(
            P(None, "chan", "slab", None, None),
            P(None, None, "chan", None, None, "slab"),
            P("chan"),
        ),
        out_specs=P(None, "chan", "slab", None, None),
        check_vma=False,
    )
```

```python
import functools

import jax
import jax.numpy as jnp
import numpy as np
from jax import lax
from jax.experimental import pallas as pl
from jax.experimental.pallas import tpu as pltpu
from jax.sharding import PartitionSpec as P

NG = 256
KM = 32
F32 = jnp.float32
BF16 = jnp.bfloat16
VMEM_LIMIT = 48 * 1024 * 1024


def kept_freqs(mode_count, grid_side):
    index = np.arange(mode_count)
    return np.where(index < mode_count // 2, index, index + grid_side - mode_count)


def angles(freq_list, grid_side):
    product = freq_list[:, None] * np.arange(grid_side)[None, :] % grid_side
    return product.astype(np.float32) * np.float32(2.0 * np.pi / grid_side)


def make_tables(chans):
    two = 2 * KM
    fwd = np.float32(1.0) / np.sqrt(np.float32(NG))
    inv = np.float32(1.0) / np.sqrt(np.float32(two))
    theta_z = angles(np.arange(KM), NG)
    theta_two = angles(kept_freqs(two, NG), NG)
    cos_z, sin_z = np.cos(theta_z), np.sin(theta_z)
    cos_t, sin_t = np.cos(theta_two), np.sin(theta_two)
    lanes = 2 * chans * KM
    fwd_z = np.zeros((chans, NG, 2, chans, KM), np.float32)
    inv_z = np.zeros((chans, 2, chans, KM, NG), np.float32)
    weight_k = np.where(np.arange(KM) == 0, 1.0, 2.0).astype(np.float32)[:, None]
    for c in range(chans):
        fwd_z[c, :, 0, c, :] = cos_z.T * fwd
        fwd_z[c, :, 1, c, :] = -sin_z.T * fwd
        inv_z[c, 0, c] = weight_k * cos_z * inv
        inv_z[c, 1, c] = -weight_k * sin_z * inv
    fwd_z = fwd_z.reshape(chans * NG, lanes)
    inv_z = inv_z.reshape(chans, lanes, NG)
    fwd_two = np.concatenate([cos_t, sin_t], 0) * fwd
    inv_two = np.concatenate([cos_t.T, sin_t.T], 1) * inv
    return tuple(jnp.asarray(t, BF16) for t in (fwd_z, fwd_two, inv_two, inv_z))


def dot(a, b):
    return jnp.dot(a, b, preferred_element_type=F32)


def turn(rows):
    half = rows.shape[-1] // 2
    return jnp.concatenate([-rows[:, half:], rows[:, :half]], axis=1)


def unturn(twice):
    two, half = twice.shape[0] // 2, twice.shape[1] // 2
    cos_part, sin_part = twice[:two], twice[two:]
    return jnp.concatenate(
        [cos_part[:, :half] + sin_part[:, half:], cos_part[:, half:] - sin_part[:, :half]], axis=1
    )


def call(kernel, cost, **kwargs):
    flops, moved = cost
    return pl.pallas_call(
        kernel,
        compiler_params=pltpu.CompilerParams(vmem_limit_bytes=VMEM_LIMIT),
        cost_estimate=pl.CostEstimate(flops=flops, bytes_accessed=moved, transcendentals=0),
        **kwargs,
    )


def forward_zy(state, sample, slabs, fwd_z, fwd_two):
    _, chans, planes, _, _ = state.shape
    two = fwd_two.shape[0] // 2
    own = two // slabs
    lanes = fwd_z.shape[1]
    step = min(planes, max(8, 16 // own))

    def kernel(state_ref, fwd_z_ref, fwd_two_ref, out_ref, coef_z):
        for x in range(step):
            plane = jnp.concatenate([state_ref[0, c, x] for c in range(chans)], axis=1)
            coef_z[x] = dot(plane, fwd_z_ref[...]).astype(BF16)
        found = []
        for x in range(step):
            modes = unturn(dot(fwd_two_ref[...], coef_z[x]))
            found.append(modes.reshape(slabs, own, lanes))
        rows = jnp.stack(found, axis=1).reshape(slabs, step * own, lanes)
        out_ref[...] = rows.astype(BF16)

    return call(
        kernel,
        (2 * planes * NG * lanes * (chans * NG + 2 * two), 2 * chans * planes * NG * NG),
        grid=(planes // step,),
        in_specs=[
            pl.BlockSpec((1, chans, step, NG, NG), lambda i: (sample, 0, i, 0, 0)),
            pl.BlockSpec(fwd_z.shape, lambda i: (0, 0)),
            pl.BlockSpec(fwd_two.shape, lambda i: (0, 0)),
        ],
        out_specs=pl.BlockSpec((slabs, step * own, lanes), lambda i: (0, i, 0)),
        out_shape=jax.ShapeDtypeStruct((slabs, planes * own, lanes), BF16),
        scratch_shapes=[pltpu.VMEM((step, NG, lanes), BF16)],
        name="forward_zy",
    )(state, fwd_z, fwd_two)


def forward_x(coef_y, me, groups, fwd_two):
    slabs, rows, lanes = coef_y.shape
    two = fwd_two.shape[0] // 2
    own = two // slabs
    half = lanes // 2
    part = two // groups

    def kernel(me_ref, coef_ref, table_ref, *refs):
        wide, found = refs[groups:]
        flat = coef_ref[...].reshape(slabs * rows, lanes).astype(F32)
        wide[0] = flat[:, :half]
        wide[1] = flat[:, half:]
        for n in range(own):
            pick = pl.ds(n, NG, stride=own)
            planes = jnp.concatenate([wide[0, pick, :], wide[1, pick, :]], axis=1)
            modes = unturn(dot(table_ref[...], planes.astype(BF16)))
            put = pl.ds(n, two, stride=own)
            found[0, put, :] = modes[:, :half]
            found[1, put, :] = modes[:, half:]
        for r in range(groups):
            start = pl.multiple_of((me_ref[0] ^ r) * part * own, part * own)
            pick = pl.ds(start, part * own)
            both = jnp.concatenate([found[0, pick, :], found[1, pick, :]], axis=1)
            refs[r][...] = both.astype(BF16)

    return call(
        kernel,
        (4 * own * two * NG * lanes, 4 * slabs * rows * lanes),
        in_specs=[pl.BlockSpec(memory_space=pltpu.SMEM)]
        + [pl.BlockSpec(memory_space=pltpu.VMEM)] * 2,
        out_specs=[pl.BlockSpec(memory_space=pltpu.VMEM)] * groups,
        out_shape=[jax.ShapeDtypeStruct((part * own, lanes), BF16)] * groups,
        scratch_shapes=[
            pltpu.VMEM((2, slabs * rows, half), F32),
            pltpu.VMEM((2, two * own, half), F32),
        ],
        name="forward_x",
    )(me, coef_y, fwd_two)


def place_weights(weights, me, chans):
    inputs, outputs, modes, _, own, kept = weights.shape
    groups = inputs // chans
    rows = modes * own
    lanes = chans * kept

    def kernel(me_ref, w_ref, out_ref):
        for g in range(groups):
            first = (me_ref[0] ^ g) * chans
            for q in range(2):
                for r in range(chans):
                    tiles = [
                        w_ref[(o + r) % chans, first + o, :, q].astype(F32).reshape(rows, kept)
                        for o in range(chans)
                    ]
                    out_ref[q, 0, g, r] = jnp.concatenate(tiles, axis=1).astype(BF16)

    return call(
        kernel,
        (2 * weights.size, 10 * weights.size),
        grid_spec=pltpu.PrefetchScalarGridSpec(
            num_scalar_prefetch=1,
            grid=(groups,),
            in_specs=[
                pl.BlockSpec(
                    (chans, outputs, modes, 2, own, kept),
                    lambda i, me_ref: (me_ref[0] ^ i, 0, 0, 0, 0, 0),
                )
            ],
            out_specs=pl.BlockSpec(
                (2, 1, groups, chans, rows, lanes), lambda i, me_ref: (0, i, 0, 0, 0, 0)
            ),
        ),
        out_shape=jax.ShapeDtypeStruct(
            (2, groups, outputs // chans, chans, rows, lanes), BF16
        ),
        name="place_weights",
    )(me, weights)


def mix(spectra, placed, kept):
    groups = len(spectra)
    rows, lanes = spectra[0].shape
    half = lanes // 2
    chans = placed.shape[3]
    step = min(rows, 32)

    def kernel(w_ref, *refs):
        total = [[jnp.zeros((step, half), F32) for _ in range(2)] for _ in range(groups)]
        for i in range(groups):
            both = refs[i][...].astype(F32)
            for r in range(chans):
                if r == 0:
                    re, im = both[:, :half], both[:, half:]
                else:
                    re = pltpu.roll(both[:, :half], half - r * kept, 1)
                    im = pltpu.roll(both[:, half:], half - r * kept, 1)
                for o in range(groups):
                    w_re = w_ref[0, i, o, r].astype(F32)
                    w_im = w_ref[1, i, o, r].astype(F32)
                    total[o][0] = total[o][0] + (re * w_re - im * w_im)
                    total[o][1] = total[o][1] + (re * w_im + im * w_re)
        for o in range(groups):
            refs[groups + o][...] = jnp.concatenate(total[o], axis=1).astype(BF16)

    return call(
        kernel,
        (8 * groups * groups * chans * rows * half, 2 * placed.size),
        grid=(rows // step,),
        in_specs=[pl.BlockSpec(placed.shape[:4] + (step, half), lambda t: (0, 0, 0, 0, t, 0))]
        + [pl.BlockSpec((step, lanes), lambda t: (t, 0))] * groups,
        out_specs=[pl.BlockSpec((step, lanes), lambda t: (t, 0))] * groups,
        out_shape=[jax.ShapeDtypeStruct((rows, lanes), BF16)] * groups,
        name="mix",
    )(placed, *spectra)


def inverse_x(mixed, me, slabs, inv_two):
    groups = len(mixed)
    rows, lanes = mixed[0].shape
    two = inv_two.shape[1] // 2
    own = groups * rows // two
    half = lanes // 2

    def kernel(me_ref, table_ref, *refs):
        out_ref, wide, found = refs[groups:]
        for r in range(groups):
            put = pl.ds(pl.multiple_of((me_ref[0] ^ r) * rows, rows), rows)
            both = refs[r][...].astype(F32)
            wide[0, put, :] = both[:, :half]
            wide[1, put, :] = both[:, half:]
        for n in range(own):
            pick = pl.ds(n, two, stride=own)
            modes = jnp.concatenate([wide[0, pick, :], wide[1, pick, :]], axis=1)
            twice = jnp.concatenate([modes, turn(modes)], axis=0).astype(BF16)
            planes = dot(table_ref[...], twice)
            put = pl.ds(n, NG, stride=own)
            found[0, put, :] = planes[:, :half]
            found[1, put, :] = planes[:, half:]
        both = jnp.concatenate([found[0], found[1]], axis=1)
        out_ref[...] = both.reshape(slabs, NG * own // slabs, lanes).astype(BF16)

    return call(
        kernel,
        (4 * own * two * NG * lanes, 4 * NG * own * lanes),
        in_specs=[pl.BlockSpec(memory_space=pltpu.SMEM)]
        + [pl.BlockSpec(memory_space=pltpu.VMEM)] * (1 + groups),
        out_specs=pl.BlockSpec(memory_space=pltpu.VMEM),
        out_shape=jax.ShapeDtypeStruct((slabs, NG * own // slabs, lanes), BF16),
        scratch_shapes=[
            pltpu.VMEM((2, two * own, half), F32),
            pltpu.VMEM((2, NG * own, half), F32),
        ],
        name="inverse_x",
    )(me, inv_two, *mixed)


def inverse_yz(back_x, shift, sample, shape, filled, inv_two, inv_z):
    slabs, rows, lanes = back_x.shape
    _, chans, planes, _, _ = shape
    two = inv_two.shape[1] // 2
    own = two // slabs
    step = min(planes, max(8, 16 // own))

    def kernel(back_ref, shift_ref, inv_two_ref, inv_z_ref, *refs):
        out_ref, back_y = refs[-2:]
        wide = back_ref[...].astype(F32)
        for x in range(step):
            modes = wide[:, x * own : (x + 1) * own, :].reshape(two, lanes)
            twice = jnp.concatenate([modes, turn(modes)], axis=0).astype(BF16)
            back_y[x] = dot(inv_two_ref[...], twice).astype(BF16)
        flat = back_y[...].reshape(step * NG, lanes)
        for c in range(chans):
            shifted = dot(flat, inv_z_ref[c]) + shift_ref[c]
            half = 0.5 * shifted
            value = half + half * lax.erf(shifted * np.float32(np.sqrt(0.5)))
            out_ref[0, c] = value.astype(BF16).reshape(step, NG, NG)

    extra = [] if filled is None else [filled]
    return call(
        kernel,
        (2 * planes * NG * (2 * two * lanes + chans * lanes * NG), 2 * chans * planes * NG * NG),
        grid=(planes // step,),
        in_specs=[
            pl.BlockSpec((slabs, step * own, lanes), lambda i: (0, i, 0)),
            pl.BlockSpec(memory_space=pltpu.SMEM),
            pl.BlockSpec(inv_two.shape, lambda i: (0, 0)),
            pl.BlockSpec(inv_z.shape, lambda i: (0, 0, 0)),
        ]
        + [pl.BlockSpec(memory_space=pl.ANY)] * len(extra),
        out_specs=pl.BlockSpec((1, chans, step, NG, NG), lambda i: (sample, 0, i, 0, 0)),
        out_shape=jax.ShapeDtypeStruct(shape, BF16),
        scratch_shapes=[pltpu.VMEM((step, NG, lanes), BF16)],
        input_output_aliases={} if filled is None else {4: 0},
        name="inverse_yz",
    )(back_x, shift, inv_two, inv_z, *extra)


def exchange(blocks, axis):
    return lax.all_to_all(blocks, axis, split_axis=0, concat_axis=0, tiled=True)


def swap(blocks, axis):
    count = len(blocks)
    return list(blocks[:1]) + [
        lax.ppermute(blocks[r], axis, [(i, i ^ r) for i in range(count)]) for r in range(1, count)
    ]


def on_device(slabs, groups, state, weights, shift):
    samples, chans = state.shape[:2]
    fwd_z, fwd_two, inv_two, inv_z = make_tables(chans)
    shift = shift.astype(F32)
    me = lax.axis_index("chan").reshape(1)
    placed = place_weights(jnp.transpose(weights, (0, 1, 2, 4, 5, 3)), me, chans)
    coef_y, back_x = [], []
    for b in range(samples):
        sent = forward_zy(state, b, slabs, fwd_z, fwd_two)
        if b == 1:
            sent, placed = lax.optimization_barrier((sent, placed))
        coef_y.append(exchange(sent, "slab"))
    for b in range(samples):
        spectra = swap(forward_x(coef_y[b], me, groups, fwd_two), "chan")
        mixed = swap(mix(spectra, placed, KM), "chan")
        back_x.append(exchange(inverse_x(mixed, me, slabs, inv_two), "slab"))
    out = None
    for b in range(samples):
        out = inverse_yz(back_x[b], shift, b, state.shape, out, inv_two, inv_z)
    return out


def solution(mesh):
    slabs, groups = mesh.shape["slab"], mesh.shape["chan"]
    return jax.shard_map(
        functools.partial(on_device, slabs, groups),
        mesh=mesh,
        in_specs=(
            P(None, "chan", "slab", None, None),
            P(None, None, "chan", None, None, "slab"),
            P("chan"),
        ),
        out_specs=P(None, "chan", "slab", None, None),
        check_vma=False,
    )
```

```python
import functools

import jax
import jax.numpy as jnp
import numpy as np
from jax import lax
from jax.experimental import pallas as pl
from jax.experimental.pallas import tpu as pltpu
from jax.sharding import PartitionSpec as P

NG = 256
KM = 32
F32 = jnp.float32
BF16 = jnp.bfloat16
VMEM_LIMIT = 48 * 1024 * 1024


def kept_freqs(mode_count, grid_side):
    index = np.arange(mode_count)
    return np.where(index < mode_count // 2, index, index + grid_side - mode_count)


def angles(freq_list, grid_side):
    product = freq_list[:, None] * np.arange(grid_side)[None, :] % grid_side
    return product.astype(np.float32) * np.float32(2.0 * np.pi / grid_side)


def make_tables(chans):
    two = 2 * KM
    fwd = np.float32(1.0) / np.sqrt(np.float32(NG))
    inv = np.float32(1.0) / np.sqrt(np.float32(two))
    theta_z = angles(np.arange(KM), NG)
    theta_two = angles(kept_freqs(two, NG), NG)
    cos_z, sin_z = np.cos(theta_z), np.sin(theta_z)
    cos_t, sin_t = np.cos(theta_two), np.sin(theta_two)
    lanes = 2 * chans * KM
    fwd_z = np.zeros((chans, NG, 2, chans, KM), np.float32)
    inv_z = np.zeros((chans, 2, chans, KM, NG), np.float32)
    weight_k = np.where(np.arange(KM) == 0, 1.0, 2.0).astype(np.float32)[:, None]
    for c in range(chans):
        fwd_z[c, :, 0, c, :] = cos_z.T * fwd
        fwd_z[c, :, 1, c, :] = -sin_z.T * fwd
        inv_z[c, 0, c] = weight_k * cos_z * inv
        inv_z[c, 1, c] = -weight_k * sin_z * inv
    fwd_z = fwd_z.reshape(chans * NG, lanes)
    inv_z = inv_z.reshape(chans, lanes, NG)
    fwd_two = np.concatenate([cos_t, sin_t], 0) * fwd
    inv_two = np.concatenate([cos_t.T, sin_t.T], 1) * inv
    return tuple(jnp.asarray(t, BF16) for t in (fwd_z, fwd_two, inv_two, inv_z))


def dot(a, b):
    return jnp.dot(a, b, preferred_element_type=F32)


def turn(rows):
    half = rows.shape[-1] // 2
    return jnp.concatenate([-rows[:, half:], rows[:, :half]], axis=1)


def unturn(twice):
    two, half = twice.shape[0] // 2, twice.shape[1] // 2
    cos_part, sin_part = twice[:two], twice[two:]
    return jnp.concatenate(
        [cos_part[:, :half] + sin_part[:, half:], cos_part[:, half:] - sin_part[:, :half]], axis=1
    )


def call(kernel, cost, **kwargs):
    flops, moved = cost
    return pl.pallas_call(
        kernel,
        compiler_params=pltpu.CompilerParams(vmem_limit_bytes=VMEM_LIMIT),
        cost_estimate=pl.CostEstimate(flops=flops, bytes_accessed=moved, transcendentals=0),
        **kwargs,
    )


def forward_zy(state, sample, slabs, fwd_z, fwd_two):
    _, chans, planes, _, _ = state.shape
    two = fwd_two.shape[0] // 2
    own = two // slabs
    lanes = fwd_z.shape[1]
    step = min(planes, max(8, 16 // own))

    def kernel(state_ref, fwd_z_ref, fwd_two_ref, out_ref, coef_z):
        for x in range(step):
            plane = jnp.concatenate([state_ref[0, c, x] for c in range(chans)], axis=1)
            coef_z[x] = dot(plane, fwd_z_ref[...]).astype(BF16)
        found = []
        for x in range(step):
            modes = unturn(dot(fwd_two_ref[...], coef_z[x]))
            found.append(modes.reshape(slabs, own, lanes))
        rows = jnp.stack(found, axis=1).reshape(slabs, step * own, lanes)
        out_ref[...] = rows.astype(BF16)

    return call(
        kernel,
        (2 * planes * NG * lanes * (chans * NG + 2 * two), 2 * chans * planes * NG * NG),
        grid=(planes // step,),
        in_specs=[
            pl.BlockSpec((1, chans, step, NG, NG), lambda i: (sample, 0, i, 0, 0)),
            pl.BlockSpec(fwd_z.shape, lambda i: (0, 0)),
            pl.BlockSpec(fwd_two.shape, lambda i: (0, 0)),
        ],
        out_specs=pl.BlockSpec((slabs, step * own, lanes), lambda i: (0, i, 0)),
        out_shape=jax.ShapeDtypeStruct((slabs, planes * own, lanes), BF16),
        scratch_shapes=[pltpu.VMEM((step, NG, lanes), BF16)],
        name="forward_zy",
    )(state, fwd_z, fwd_two)


def forward_x(coef_y, me, groups, fwd_two):
    slabs, rows, lanes = coef_y.shape
    two = fwd_two.shape[0] // 2
    own = two // slabs
    half = lanes // 2
    part = two // groups

    def kernel(me_ref, coef_ref, table_ref, *refs):
        wide, found = refs[groups:]
        flat = coef_ref[...].reshape(slabs * rows, lanes).astype(F32)
        wide[0] = flat[:, :half]
        wide[1] = flat[:, half:]
        for n in range(own):
            pick = pl.ds(n, NG, stride=own)
            planes = jnp.concatenate([wide[0, pick, :], wide[1, pick, :]], axis=1)
            modes = unturn(dot(table_ref[...], planes.astype(BF16)))
            put = pl.ds(n, two, stride=own)
            found[0, put, :] = modes[:, :half]
            found[1, put, :] = modes[:, half:]
        for r in range(groups):
            start = pl.multiple_of((me_ref[0] ^ r) * part * own, part * own)
            pick = pl.ds(start, part * own)
            both = jnp.concatenate([found[0, pick, :], found[1, pick, :]], axis=1)
            refs[r][...] = both.astype(BF16)

    return call(
        kernel,
        (4 * own * two * NG * lanes, 4 * slabs * rows * lanes),
        in_specs=[pl.BlockSpec(memory_space=pltpu.SMEM)]
        + [pl.BlockSpec(memory_space=pltpu.VMEM)] * 2,
        out_specs=[pl.BlockSpec(memory_space=pltpu.VMEM)] * groups,
        out_shape=[jax.ShapeDtypeStruct((part * own, lanes), BF16)] * groups,
        scratch_shapes=[
            pltpu.VMEM((2, slabs * rows, half), F32),
            pltpu.VMEM((2, two * own, half), F32),
        ],
        name="forward_x",
    )(me, coef_y, fwd_two)


def place_weights(weights, me, chans):
    inputs, outputs, modes, _, own, kept = weights.shape
    groups = inputs // chans
    rows = modes * own
    lanes = chans * kept

    def kernel(me_ref, w_ref, out_ref):
        for g in range(groups):
            first = (me_ref[0] ^ g) * chans
            for q in range(2):
                for r in range(chans):
                    tiles = [
                        w_ref[(o + r) % chans, first + o, :, q].astype(F32).reshape(rows, kept)
                        for o in range(chans)
                    ]
                    out_ref[q, 0, g, r] = jnp.concatenate(tiles, axis=1).astype(BF16)

    return call(
        kernel,
        (2 * weights.size, 10 * weights.size),
        grid_spec=pltpu.PrefetchScalarGridSpec(
            num_scalar_prefetch=1,
            grid=(groups,),
            in_specs=[
                pl.BlockSpec(
                    (chans, outputs, modes, 2, own, kept),
                    lambda i, me_ref: (me_ref[0] ^ i, 0, 0, 0, 0, 0),
                )
            ],
            out_specs=pl.BlockSpec(
                (2, 1, groups, chans, rows, lanes), lambda i, me_ref: (0, i, 0, 0, 0, 0)
            ),
        ),
        out_shape=jax.ShapeDtypeStruct(
            (2, groups, outputs // chans, chans, rows, lanes), BF16
        ),
        name="place_weights",
    )(me, weights)


def mix(spectra, placed, kept):
    groups = len(spectra)
    rows, lanes = spectra[0].shape
    half = lanes // 2
    chans = placed.shape[3]
    step = min(rows, 32)

    def kernel(w_ref, *refs):
        total = [[jnp.zeros((step, half), F32) for _ in range(2)] for _ in range(groups)]
        for i in range(groups):
            both = refs[i][...].astype(F32)
            for r in range(chans):
                if r == 0:
                    re, im = both[:, :half], both[:, half:]
                else:
                    re = pltpu.roll(both[:, :half], half - r * kept, 1)
                    im = pltpu.roll(both[:, half:], half - r * kept, 1)
                for o in range(groups):
                    w_re = w_ref[0, i, o, r].astype(F32)
                    w_im = w_ref[1, i, o, r].astype(F32)
                    total[o][0] = total[o][0] + (re * w_re - im * w_im)
                    total[o][1] = total[o][1] + (re * w_im + im * w_re)
        for o in range(groups):
            refs[groups + o][...] = jnp.concatenate(total[o], axis=1).astype(BF16)

    return call(
        kernel,
        (8 * groups * groups * chans * rows * half, 2 * placed.size),
        grid=(rows // step,),
        in_specs=[pl.BlockSpec(placed.shape[:4] + (step, half), lambda t: (0, 0, 0, 0, t, 0))]
        + [pl.BlockSpec((step, lanes), lambda t: (t, 0))] * groups,
        out_specs=[pl.BlockSpec((step, lanes), lambda t: (t, 0))] * groups,
        out_shape=[jax.ShapeDtypeStruct((rows, lanes), BF16)] * groups,
        name="mix",
    )(placed, *spectra)


def inverse_x(mixed, me, slabs, inv_two):
    groups = len(mixed)
    rows, lanes = mixed[0].shape
    two = inv_two.shape[1] // 2
    own = groups * rows // two
    half = lanes // 2

    def kernel(me_ref, table_ref, *refs):
        out_ref, wide, found = refs[groups:]
        for r in range(groups):
            put = pl.ds(pl.multiple_of((me_ref[0] ^ r) * rows, rows), rows)
            both = refs[r][...].astype(F32)
            wide[0, put, :] = both[:, :half]
            wide[1, put, :] = both[:, half:]
        for n in range(own):
            pick = pl.ds(n, two, stride=own)
            modes = jnp.concatenate([wide[0, pick, :], wide[1, pick, :]], axis=1)
            twice = jnp.concatenate([modes, turn(modes)], axis=0).astype(BF16)
            planes = dot(table_ref[...], twice)
            put = pl.ds(n, NG, stride=own)
            found[0, put, :] = planes[:, :half]
            found[1, put, :] = planes[:, half:]
        both = jnp.concatenate([found[0], found[1]], axis=1)
        out_ref[...] = both.reshape(slabs, NG * own // slabs, lanes).astype(BF16)

    return call(
        kernel,
        (4 * own * two * NG * lanes, 4 * NG * own * lanes),
        in_specs=[pl.BlockSpec(memory_space=pltpu.SMEM)]
        + [pl.BlockSpec(memory_space=pltpu.VMEM)] * (1 + groups),
        out_specs=pl.BlockSpec(memory_space=pltpu.VMEM),
        out_shape=jax.ShapeDtypeStruct((slabs, NG * own // slabs, lanes), BF16),
        scratch_shapes=[
            pltpu.VMEM((2, two * own, half), F32),
            pltpu.VMEM((2, NG * own, half), F32),
        ],
        name="inverse_x",
    )(me, inv_two, *mixed)


def inverse_yz(back_x, shift, sample, shape, filled, inv_two, inv_z):
    slabs, rows, lanes = back_x.shape
    _, chans, planes, _, _ = shape
    two = inv_two.shape[1] // 2
    own = two // slabs
    step = min(planes, max(8, 16 // own))

    def kernel(back_ref, shift_ref, inv_two_ref, inv_z_ref, *refs):
        out_ref, back_y = refs[-2:]
        wide = back_ref[...].astype(F32)
        for x in range(step):
            modes = wide[:, x * own : (x + 1) * own, :].reshape(two, lanes)
            twice = jnp.concatenate([modes, turn(modes)], axis=0).astype(BF16)
            back_y[x] = dot(inv_two_ref[...], twice).astype(BF16)
        flat = back_y[...].reshape(step * NG, lanes)
        for c in range(chans):
            shifted = dot(flat, inv_z_ref[c]) + shift_ref[c]
            half = 0.5 * shifted
            value = half + half * lax.erf(shifted * np.float32(np.sqrt(0.5)))
            out_ref[0, c] = value.astype(BF16).reshape(step, NG, NG)

    extra = [] if filled is None else [filled]
    return call(
        kernel,
        (2 * planes * NG * (2 * two * lanes + chans * lanes * NG), 2 * chans * planes * NG * NG),
        grid=(planes // step,),
        in_specs=[
            pl.BlockSpec((slabs, step * own, lanes), lambda i: (0, i, 0)),
            pl.BlockSpec(memory_space=pltpu.SMEM),
            pl.BlockSpec(inv_two.shape, lambda i: (0, 0)),
            pl.BlockSpec(inv_z.shape, lambda i: (0, 0, 0)),
        ]
        + [pl.BlockSpec(memory_space=pl.ANY)] * len(extra),
        out_specs=pl.BlockSpec((1, chans, step, NG, NG), lambda i: (sample, 0, i, 0, 0)),
        out_shape=jax.ShapeDtypeStruct(shape, BF16),
        scratch_shapes=[pltpu.VMEM((step, NG, lanes), BF16)],
        input_output_aliases={} if filled is None else {4: 0},
        name="inverse_yz",
    )(back_x, shift, inv_two, inv_z, *extra)


def exchange(blocks, axis):
    return lax.all_to_all(blocks, axis, split_axis=0, concat_axis=0, tiled=True)


def swap(blocks, axis):
    count = len(blocks)
    return list(blocks[:1]) + [
        lax.ppermute(blocks[r], axis, [(i, i ^ r) for i in range(count)]) for r in range(1, count)
    ]


def on_device(slabs, groups, state, weights, shift):
    samples, chans = state.shape[:2]
    fwd_z, fwd_two, inv_two, inv_z = make_tables(chans)
    shift = shift.astype(F32)
    fwd_z, fwd_two = (pltpu.with_memory_space_constraint(t, pltpu.HBM) for t in (fwd_z, fwd_two))
    me = lax.axis_index("chan").reshape(1)
    placed = place_weights(jnp.transpose(weights, (0, 1, 2, 4, 5, 3)), me, chans)
    coef_y, back_x = [], []
    for b in range(samples):
        sent = forward_zy(state, b, slabs, fwd_z, fwd_two)
        if b == 1:
            sent, placed = lax.optimization_barrier((sent, placed))
        coef_y.append(exchange(sent, "slab"))
    for b in range(samples):
        spectra = swap(forward_x(coef_y[b], me, groups, fwd_two), "chan")
        mixed = swap(mix(spectra, placed, KM), "chan")
        back_x.append(exchange(inverse_x(mixed, me, slabs, inv_two), "slab"))
    out = None
    for b in range(samples):
        out = inverse_yz(back_x[b], shift, b, state.shape, out, inv_two, inv_z)
    return out


def solution(mesh):
    slabs, groups = mesh.shape["slab"], mesh.shape["chan"]
    return jax.shard_map(
        functools.partial(on_device, slabs, groups),
        mesh=mesh,
        in_specs=(
            P(None, "chan", "slab", None, None),
            P(None, None, "chan", None, None, "slab"),
            P("chan"),
        ),
        out_specs=P(None, "chan", "slab", None, None),
        check_vma=False,
    )
```
